32 devices in a mesh: groups: 2 (over y), gx: 4 (over x, core), gy: 4 (over z).
Axes of the slice: x: 2, y: 2, z: 4, core: 2. Of those that a mesh axis runs over, the one named last changes fastest.
Arguments:
- layer_input: bfloat16 [256, 16384], P(('groups', 'gx'), 'gy'), parts along dimension 0, may hold values from -32 to 32, as said below
- attn_context: bfloat16 [256, 8192], P(('groups', 'gx'), 'gy'), parts along dimension 0, may hold values from -6 to 6
- ffn_hidden: bfloat16 [256, 26624], P(('groups', 'gx'), 'gy'), parts along dimension 0, may hold values from -6 to 6
- norm_gain: float32 [16384], replicated, may hold values from 0.1 to 1.9
- w_query: bfloat16 [16384, 8192], P('gx', 'gy'), may hold values from -0.046875 to 0.046875
- w_keyval: bfloat16 [16384, 1024], P('gx', 'gy'), may hold values from -0.046875 to 0.046875
- w_out: bfloat16 [8192, 16384], P('gx', 'gy'), may hold values from -0.0625 to 0.0625
- w_down: bfloat16 [26624, 16384], P('gx', 'gy'), may hold values from -0.0390625 to 0.0390625
Outputs:
- queries: bfloat16 [256, 8192], P(('groups', 'gx'), 'gy'), parts along dimension 0
- keys_values: bfloat16 [256, 1024], P(('groups', 'gx'), 'gy'), parts along dimension 0
- block_output: bfloat16 [256, 16384], P(('groups', 'gx'), 'gy'), parts along dimension 0
The draws below stay inside these ranges and needn't reach their ends.
There are 2 independent parts, one for each index of `groups`. The reference program is written for one: setup_inputs(seed, part) draws one part's arguments, and reference() takes and returns one part's arrays. A program takes and returns all parts, laid end to end along the dimension named above; an argument that names none is the same for every part. Nothing has to cross between parts.
Inputs may be any that keep to these rules, and one draw needn't show every extreme that they name: `layer_input`: the layer's input.
All inputs are finite; a program needn't handle non-finite values.
Results may differ from the reference program's by a relative error of at most 0.005.
Values may be sent and summed in bfloat16 or wider, within the bound.
No kernel may reach another device: no remote copies, remote signals or barrier semaphores. Data moves between devices by JAX's collectives and lax.ppermute only.
A program may use at most 192 MiB of HBM per device.

```python
import jax
import jax.numpy as jnp
from jax import lax

D = 16384
FW = 26624
HQ = 8192
KVW = 512
ROWS = 128


def draw_layer_input(key, part):
    key = jax.random.fold_in(key, 11)
    key_base, key_rows, key_cols = jax.random.split(key, 3)
    position = jnp.arange(D, dtype=jnp.float32) / D
    base = jnp.clip(jax.random.normal(key_base, (ROWS, D), jnp.float32), -5.0, 5.0)
    row_scale = jnp.exp(jax.random.uniform(key_rows, (ROWS, 1), jnp.float32, -1.204, 1.098))
    col_scale = jnp.exp(1.0986 * (position - 0.5)) * jax.random.uniform(key_cols, (D,), jnp.float32, 0.6, 1.4)
    return (base * row_scale * col_scale).astype(jnp.bfloat16)


def steps_of(key, shape, cuts, least, top_value):
    gain = 1.0
    for axis_at, blocks in cuts:
        draws = jax.random.uniform(jax.random.fold_in(jax.random.fold_in(key, 6), axis_at), (blocks,), jnp.float32, least / len(cuts), top_value / len(cuts))
        gain = gain * jnp.repeat(jnp.exp(draws), shape[axis_at] // blocks).reshape((-1,) + (1,) * (len(shape) - 1 - axis_at))
    return gain


def normal_values(own_key, shape, deviation, reach, cuts=(), kind=jnp.bfloat16):
    drawn = deviation * jax.random.normal(own_key, shape, jnp.float32)
    if cuts:
        drawn = drawn * steps_of(own_key, shape, cuts, -0.22, 0.18)
    return jnp.clip(drawn, -reach, reach).astype(kind)


def setup_inputs(seed: int = 0, part: int = 0) -> dict:
    splits = jax.random.split(jax.random.key(seed), 9)
    own_keys = jax.random.split(jax.random.fold_in(splits[8], part), 9)
    layer_input = draw_layer_input(jax.random.fold_in(jax.random.fold_in(splits[8], part), 71), part)
    attn_context = normal_values(own_keys[1], (ROWS, HQ), 1.0, 6.0, ((0, 4), (1, 4)))
    ffn_hidden = normal_values(own_keys[2], (ROWS, FW), 1.0, 6.0, ((0, 4), (1, 4)))
    norm_gain = jnp.clip(1.0 + 0.18 * jax.random.normal(splits[3], (D,), jnp.float32), 0.1, 1.9)
    w_query = normal_values(splits[4], (D, HQ), D ** -0.5, 0.046875, ((0, 4), (1, 4)))
    w_keyval = normal_values(splits[5], (D, 2 * KVW), D ** -0.5, 0.046875, ((0, 4), (1, 4)))
    w_out = normal_values(splits[6], (HQ, D), HQ ** -0.5, 0.0625, ((0, 4), (1, 4)))
    w_down = normal_values(splits[7], (FW, D), FW ** -0.5, 0.0390625, ((0, 4), (1, 4)))
    return dict(layer_input=layer_input, attn_context=attn_context, ffn_hidden=ffn_hidden, norm_gain=norm_gain, w_query=w_query, w_keyval=w_keyval, w_out=w_out, w_down=w_down)


def reference(layer_input, attn_context, ffn_hidden, norm_gain, w_query, w_keyval, w_out, w_down):
    input_float = layer_input.astype(jnp.float32)
    mean_square = lax.optimization_barrier(jnp.mean(input_float * input_float, axis=1, keepdims=True))
    normed = (input_float * lax.rsqrt(mean_square + 1e-05) * norm_gain.astype(jnp.float32)).astype(jnp.bfloat16)
    queries = jnp.dot(normed, w_query, preferred_element_type=jnp.float32).astype(jnp.bfloat16)
    keys_values = jnp.dot(normed, w_keyval, preferred_element_type=jnp.float32).astype(jnp.bfloat16)
    attn_part = jnp.dot(attn_context, w_out, preferred_element_type=jnp.float32)
    ffn_part = jnp.dot(ffn_hidden, w_down, preferred_element_type=jnp.float32)
    block_output = (input_float + attn_part + ffn_part).astype(jnp.bfloat16)
    return (queries, keys_values, block_output)
```

```python
import jax
import jax.numpy as jnp
from jax import lax
from jax.sharding import PartitionSpec as P

norm_epsilon = 1e-05


def solution(mesh):
    nx, ny = mesh.shape["gx"], mesh.shape["gy"]
    ratio = nx // ny
    assert nx == ratio * ny

    def routes(shift, turn):
        pairs = []
        for gx in range(nx):
            for gy in range(ny):
                piece = (turn + gx) % ratio
                target = (gy * ratio + piece, (gx // ratio + shift) % ny)
                pairs.append((gx * ny + gy, target[0] * ny + target[1]))
        return pairs

    steps = [(shift, turn, routes(shift, turn)) for shift in range(ny) for turn in range(ratio)]

    def spread(block):
        gx = lax.axis_index("gx")
        width = block.shape[1] // ratio
        parts = []
        for shift, turn, pairs in steps:
            piece = block
            if ratio > 1:
                piece = lax.dynamic_slice_in_dim(block, (turn + gx) % ratio * width, width, axis=1)
            parts.append(lax.ppermute(piece, ("gx", "gy"), pairs))
        return jnp.concatenate(parts, axis=0)

    def row_block_of(step):
        shift, turn, _ = steps[step]
        gx, gy = lax.axis_index("gx"), lax.axis_index("gy")
        return (gy - shift) % ny * ratio + (gx % ratio - turn) % ratio

    def step_of(owner):
        gx, gy = lax.axis_index("gx"), lax.axis_index("gy")
        return (gy - owner // ratio) % ny * ratio + (gx % ratio - owner % ratio) % ratio

    def sum_over_gx(partial, rows):
        gx = lax.axis_index("gx")

        def rows_of(owner):
            return lax.dynamic_slice_in_dim(partial, step_of(owner) * rows, rows, axis=0)

        total = rows_of(gx)
        for hop in range(1, nx):
            pairs = [(i, (i + hop) % nx) for i in range(nx)]
            sent = rows_of((gx + hop) % nx).astype(jnp.bfloat16)
            total = total + lax.ppermute(sent, "gx", pairs).astype(jnp.float32)
        return total

    def local(layer_input, attn_context, ffn_hidden, norm_gain, w_query, w_keyval, w_out, w_down):
        rows = layer_input.shape[0]
        model_width = norm_gain.shape[0]
        depth = w_query.shape[0]
        gx = lax.axis_index("gx")

        input_float = layer_input.astype(jnp.float32)
        row_sums = jnp.sum(input_float * input_float, axis=1)
        all_sums = lax.all_gather(row_sums, ("gx", "gy"), axis=0, tiled=False)
        all_sums = jnp.sum(all_sums.reshape(nx, ny, rows), axis=1)

        column_context = spread(attn_context)
        column_hidden = spread(ffn_hidden)
        column_input = spread(layer_input)

        block_part = jnp.dot(column_context, w_out, preferred_element_type=jnp.float32)
        block_part = block_part + jnp.dot(column_hidden, w_down, preferred_element_type=jnp.float32)
        block_sum = sum_over_gx(block_part, rows)

        order = jnp.stack([row_block_of(step) for step in range(len(steps))])
        mean_square = jnp.take(all_sums, order, axis=0).reshape(nx * rows, 1) / model_width
        gain = lax.dynamic_slice_in_dim(norm_gain, gx * depth, depth)
        normed = (column_input.astype(jnp.float32) * lax.rsqrt(mean_square + norm_epsilon) * gain).astype(jnp.bfloat16)
        query_part = jnp.dot(normed, w_query, preferred_element_type=jnp.float32)
        keyval_part = jnp.dot(normed, w_keyval, preferred_element_type=jnp.float32)
        queries = sum_over_gx(query_part, rows).astype(jnp.bfloat16)
        keys_values = sum_over_gx(keyval_part, rows).astype(jnp.bfloat16)
        return (queries, keys_values, (input_float + block_sum).astype(jnp.bfloat16))

    return jax.shard_map(
        local,
        mesh=mesh,
        in_specs=(
            P(("groups", "gx"), "gy"),
            P(("groups", "gx"), "gy"),
            P(("groups", "gx"), "gy"),
            P(),
            P("gx", "gy"),
            P("gx", "gy"),
            P("gx", "gy"),
            P("gx", "gy"),
        ),
        out_specs=(P(("groups", "gx"), "gy"), P(("groups", "gx"), "gy"), P(("groups", "gx"), "gy")),
        check_vma=False,
    )
```

```python
import jax
import jax.numpy as jnp
from jax import lax
from jax.sharding import PartitionSpec as P

norm_epsilon = 1e-05


def after(value, *others):
    return lax.optimization_barrier((value, others))[0]


def dot(left, right):
    return jnp.dot(left, right, preferred_element_type=jnp.float32)


def flip(value, axis, bit):
    return lax.ppermute(value, axis, [(i, i ^ bit) for i in range(lax.axis_size(axis))])


slots = (0, 2, 1, 3)


def solution(mesh):
    nx, ny = mesh.shape["gx"], mesh.shape["gy"]
    square = nx == 4 and ny == 4

    def over_z(block):
        return block, flip(block, "gy", 2)

    def over_x(pair):
        block, far = pair
        mine = lax.axis_index("gx") // 2 == lax.axis_index("gy") // 2
        keep, give = jnp.where(mine, block, far), jnp.where(mine, far, block)
        return keep, flip(give, "gx", 2)

    def over_near_z(pair):
        keep = jnp.concatenate(pair)
        return keep, flip(keep, "gy", 1)

    def over_cores(pair):
        keep, near = pair
        mine = lax.axis_index("gx") % 2 == lax.axis_index("gy") % 2
        keep, give = jnp.where(mine, keep, near), jnp.where(mine, near, keep)
        return keep, flip(give, "gx", 1)

    def gather_plain(block):
        wide = lax.all_gather(block, "gy", axis=1, tiled=True)
        return lax.all_to_all(wide, "gx", split_axis=1, concat_axis=0, tiled=True)

    def sum_over_gx(partial, rows):
        if not square:
            return partial, lax.psum_scatter(partial, "gx", scatter_dimension=0, tiled=True)
        give = partial[2 * rows :]
        pair = partial[: 2 * rows] + flip(give.astype(jnp.bfloat16), "gx", 1).astype(jnp.float32)
        return pair, pair[:rows] + flip(pair[rows:].astype(jnp.bfloat16), "gx", 2).astype(jnp.float32)

    def sum_over_gy(value):
        if not square:
            return lax.psum(value, "gy")
        value = value + flip(value, "gy", 1)
        return value + flip(value, "gy", 2)

    def local(layer_input, attn_context, ffn_hidden, norm_gain, w_query, w_keyval, w_out, w_down):
        rows, feat_width = layer_input.shape
        model_width = norm_gain.shape[0]

        input_float = layer_input.astype(jnp.float32)
        row_sums = sum_over_gy(jnp.sum(input_float * input_float, axis=1))
        scale = lax.rsqrt(row_sums / model_width + norm_epsilon)
        gain = lax.dynamic_slice_in_dim(norm_gain, lax.axis_index("gy") * feat_width, feat_width)
        normed = (input_float * scale[:, None] * gain).astype(jnp.bfloat16)

        if square:
            half = ffn_hidden.shape[1] // 2
            first, second = ffn_hidden[:, :half], ffn_hidden[:, half:]
            context, first = over_z(attn_context), over_z(first)
            second = over_z(after(second, context[1]))
            context = over_x(context)
            normed = over_z(normed)
            first = over_x(first)
            context = over_near_z(context)
            context = over_cores(context)
            first = over_near_z(first)
            second = over_x(second)
            ready = jnp.concatenate(after(context, normed[1]))
            block_part = dot(ready, w_out)
            first = over_cores(first)
            normed = over_x(normed)
            second = over_near_z(second)
            ready = jnp.concatenate(after(first, block_part))
            block_part += dot(ready, w_down[:half])
            second = over_cores(after(second, block_part))
            normed = over_near_z(normed)
            ready = jnp.concatenate(after(second, block_part))
            block_part += dot(ready, w_down[half:])
            normed = jnp.concatenate(over_cores(normed))
            normed = after(normed, block_part)
        else:
            context, hidden, normed = gather_plain(attn_context), gather_plain(ffn_hidden), gather_plain(normed)
            block_part = dot(context, w_out) + dot(hidden, w_down)
        paired, block_sum = sum_over_gx(block_part, rows)
        normed = after(normed, paired)

        query_part, keyval_part = dot(normed, w_query), dot(normed, w_keyval)
        heads = sum_over_gx(jnp.concatenate([query_part, keyval_part], axis=1), rows)[1].astype(jnp.bfloat16)
        split = w_query.shape[1]
        return (heads[:, :split], heads[:, split:], (input_float + block_sum).astype(jnp.bfloat16))

    return jax.shard_map(
        local,
        mesh=mesh,
        in_specs=(
            P(("groups", "gx"), "gy"),
            P(("groups", "gx"), "gy"),
            P(("groups", "gx"), "gy"),
            P(),
            P("gx", "gy"),
            P("gx", "gy"),
            P("gx", "gy"),
            P("gx", "gy"),
        ),
        out_specs=(P(("groups", "gx"), "gy"), P(("groups", "gx"), "gy"), P(("groups", "gx"), "gy")),
        check_vma=False,
    )
```

```python
import jax
import jax.numpy as jnp
from jax import lax
from jax.sharding import PartitionSpec as P

norm_epsilon = 1e-05


def after(value, *others):
    return lax.optimization_barrier((value, others))[0]


def dot(left, right):
    return jnp.dot(left, right, preferred_element_type=jnp.float32)


def flip(value, axis, bit):
    return lax.ppermute(value, axis, [(i, i ^ bit) for i in range(lax.axis_size(axis))])


slots = (0, 2, 1, 3)


def solution(mesh):
    nx, ny = mesh.shape["gx"], mesh.shape["gy"]
    square = nx == 4 and ny == 4

    def over_z(block):
        return block, flip(block, "gy", 2)

    def over_x(pair):
        block, far = pair
        mine = lax.axis_index("gx") // 2 == lax.axis_index("gy") // 2
        keep, give = jnp.where(mine, block, far), jnp.where(mine, far, block)
        return keep, flip(give, "gx", 2)

    def over_near_z(pair):
        keep = jnp.concatenate(pair)
        return keep, flip(keep, "gy", 1)

    def over_cores(pair):
        keep, near = pair
        mine = lax.axis_index("gx") % 2 == lax.axis_index("gy") % 2
        keep, give = jnp.where(mine, keep, near), jnp.where(mine, near, keep)
        return keep, flip(give, "gx", 1)

    def gather_plain(block):
        wide = lax.all_gather(block, "gy", axis=1, tiled=True)
        return lax.all_to_all(wide, "gx", split_axis=1, concat_axis=0, tiled=True)

    def sum_over_gx(partial, rows):
        if not square:
            return partial, lax.psum_scatter(partial, "gx", scatter_dimension=0, tiled=True)
        give = partial[2 * rows :]
        pair = partial[: 2 * rows] + flip(give.astype(jnp.bfloat16), "gx", 1).astype(jnp.float32)
        return pair, pair[:rows] + flip(pair[rows:].astype(jnp.bfloat16), "gx", 2).astype(jnp.float32)

    def local(layer_input, attn_context, ffn_hidden, norm_gain, w_query, w_keyval, w_out, w_down):
        rows, feat_width = layer_input.shape
        model_width = norm_gain.shape[0]

        input_float = layer_input.astype(jnp.float32)
        gain = lax.dynamic_slice_in_dim(norm_gain, lax.axis_index("gy") * feat_width, feat_width)
        own_sums = jnp.sum(input_float * input_float, axis=1)

        def normalise(row_sums):
            scale = lax.rsqrt(row_sums / model_width + norm_epsilon)
            return (input_float * scale[:, None] * gain).astype(jnp.bfloat16)

        if square:
            half = ffn_hidden.shape[1] // 2
            first, second = ffn_hidden[:, :half], ffn_hidden[:, half:]
            context, first = over_z(attn_context), over_z(first)
            sums = own_sums + flip(own_sums, "gy", 1)
            second = over_z(after(second, context[1]))
            sums = sums + flip(after(sums, context[1]), "gy", 2)
            context = over_x(context)
            normed = normalise(sums)
            ready_norm = normed
            normed = over_z(after(normed, first[1]))
            first = over_x(first)
            context = over_cores(over_near_z(context))
            arrived = first[1]
            first = over_near_z(first)
            block_part = dot(jnp.concatenate(after(context, arrived, ready_norm)), w_out)
            second = over_x(after(second, block_part))
            normed = over_x(after(normed, block_part))
            arrived = second[1]
            second = over_near_z(second)
            first = over_cores(after(first, arrived))
            block_part += dot(jnp.concatenate(after(first, arrived)), w_down[:half])
            normed = over_near_z(after(normed, block_part))
            second = over_cores(after(second, block_part))
            block_part += dot(jnp.concatenate(second), w_down[half:])
            normed = jnp.concatenate(over_cores(after(normed, block_part)))
        else:
            normed = gather_plain(normalise(lax.psum(own_sums, "gy")))
            context, hidden = gather_plain(attn_context), gather_plain(ffn_hidden)
            block_part = dot(context, w_out) + dot(hidden, w_down)
        paired, block_sum = sum_over_gx(block_part, rows)
        normed = after(normed, paired)

        pieces = 2 if square else 1
        width = w_query.shape[1] // pieces
        heads = []
        for i in range(pieces):
            columns = dot(normed, w_query[:, i * width : (i + 1) * width])
            if i == 0:
                columns = jnp.concatenate([columns, dot(normed, w_keyval)], axis=1)
                normed = after(normed, columns, block_sum)
            heads.append(sum_over_gx(columns, rows)[1].astype(jnp.bfloat16))
        queries = jnp.concatenate([heads[0][:, :width], *heads[1:]], axis=1)
        return (queries, heads[0][:, width:], (input_float + block_sum).astype(jnp.bfloat16))

    return jax.shard_map(
        local,
        mesh=mesh,
        in_specs=(
            P(("groups", "gx"), "gy"),
            P(("groups", "gx"), "gy"),
            P(("groups", "gx"), "gy"),
            P(),
            P("gx", "gy"),
            P("gx", "gy"),
            P("gx", "gy"),
            P("gx", "gy"),
        ),
        out_specs=(P(("groups", "gx"), "gy"), P(("groups", "gx"), "gy"), P(("groups", "gx"), "gy")),
        check_vma=False,
    )
```

```python
import jax
import jax.numpy as jnp
from jax import lax
from jax.sharding import PartitionSpec as P

norm_epsilon = 1e-05


def after(value, *others):
    return lax.optimization_barrier((value, others))[0]


def dot(left, right):
    return jnp.dot(left, right, preferred_element_type=jnp.float32)


def flip(value, axis, bit):
    return lax.ppermute(value, axis, [(i, i ^ bit) for i in range(lax.axis_size(axis))])


slots = (0, 2, 1, 3)


def solution(mesh):
    nx, ny = mesh.shape["gx"], mesh.shape["gy"]
    square = nx == 4 and ny == 4

    def over_z(block):
        return block, flip(block, "gy", 2)

    def over_x(pair):
        block, far = pair
        mine = lax.axis_index("gx") // 2 == lax.axis_index("gy") // 2
        keep, give = jnp.where(mine, block, far), jnp.where(mine, far, block)
        return keep, flip(give, "gx", 2)

    def over_near_z(pair):
        keep = jnp.concatenate(pair)
        return keep, flip(keep, "gy", 1)

    def over_cores(pair):
        keep, near = pair
        mine = lax.axis_index("gx") % 2 == lax.axis_index("gy") % 2
        keep, give = jnp.where(mine, keep, near), jnp.where(mine, near, keep)
        return keep, flip(give, "gx", 1)

    def gather_plain(block):
        wide = lax.all_gather(block, "gy", axis=1, tiled=True)
        return lax.all_to_all(wide, "gx", split_axis=1, concat_axis=0, tiled=True)

    def sum_over_gx(partial, rows):
        if not square:
            return partial, lax.psum_scatter(partial, "gx", scatter_dimension=0, tiled=True)
        give = partial[2 * rows :]
        pair = partial[: 2 * rows] + flip(give.astype(jnp.bfloat16), "gx", 1).astype(jnp.float32)
        return pair, pair[:rows] + flip(pair[rows:].astype(jnp.bfloat16), "gx", 2).astype(jnp.float32)

    def local(layer_input, attn_context, ffn_hidden, norm_gain, w_query, w_keyval, w_out, w_down):
        rows, feat_width = layer_input.shape
        model_width = norm_gain.shape[0]

        input_float = layer_input.astype(jnp.float32)
        gain = lax.dynamic_slice_in_dim(norm_gain, lax.axis_index("gy") * feat_width, feat_width)
        own_sums = jnp.sum(input_float * input_float, axis=1)

        def normalise(row_sums):
            scale = lax.rsqrt(row_sums / model_width + norm_epsilon)
            return (input_float * scale[:, None] * gain).astype(jnp.bfloat16)

        if square:
            half = ffn_hidden.shape[1] // 2
            first, second = ffn_hidden[:, :half], ffn_hidden[:, half:]
            context, first = over_z(attn_context), over_z(first)
            sums = own_sums + flip(own_sums, "gy", 1)
            second = over_z(after(second, context[1]))
            sums = sums + flip(after(sums, context[1]), "gy", 2)
            context = over_x(context)
            normed = normalise(sums)
            ready_norm = normed
            normed = over_z(after(normed, second[1]))
            first = over_x(first)
            context = over_near_z(context)
            arrived = first[1]
            first = over_near_z(first)
            context = over_cores(context)
            block_part = dot(jnp.concatenate(after(context, arrived, ready_norm, second[1])), w_out)
            second = over_x(second)
            normed = over_x(after(normed, block_part))
            arrived = second[1]
            second = over_near_z(second)
            first = over_cores(after(first, arrived, block_part))
            block_part += dot(jnp.concatenate(after(first, arrived)), w_down[:half])
            normed = over_near_z(after(normed, block_part))
            second = over_cores(after(second, block_part))
            block_part += dot(jnp.concatenate(second), w_down[half:])
            normed = jnp.concatenate(over_cores(after(normed, block_part)))
        else:
            normed = gather_plain(normalise(lax.psum(own_sums, "gy")))
            context, hidden = gather_plain(attn_context), gather_plain(ffn_hidden)
            block_part = dot(context, w_out) + dot(hidden, w_down)
        paired, block_sum = sum_over_gx(block_part, rows)
        normed = after(normed, paired)

        pieces = 2 if square else 1
        width = w_query.shape[1] // pieces
        heads = []
        for i in range(pieces):
            columns = dot(normed, w_query[:, i * width : (i + 1) * width])
            if i == 0:
                columns = jnp.concatenate([columns, dot(normed, w_keyval)], axis=1)
                normed = after(normed, columns, block_sum)
            heads.append(sum_over_gx(columns, rows)[1].astype(jnp.bfloat16))
        queries = jnp.concatenate([heads[0][:, :width], *heads[1:]], axis=1)
        return (queries, heads[0][:, width:], (input_float + block_sum).astype(jnp.bfloat16))

    return jax.shard_map(
        local,
        mesh=mesh,
        in_specs=(
            P(("groups", "gx"), "gy"),
            P(("groups", "gx"), "gy"),
            P(("groups", "gx"), "gy"),
            P(),
            P("gx", "gy"),
            P("gx", "gy"),
            P("gx", "gy"),
            P("gx", "gy"),
        ),
        out_specs=(P(("groups", "gx"), "gy"), P(("groups", "gx"), "gy"), P(("groups", "gx"), "gy")),
        check_vma=False,
    )
```

```python
import jax
import jax.numpy as jnp
from jax import lax
from jax.sharding import PartitionSpec as P

norm_epsilon = 1e-05


def after(value, *others):
    return lax.optimization_barrier((value, others))[0]


def dot(left, right):
    return jnp.dot(left, right, preferred_element_type=jnp.float32)


def flip(value, axis, bit):
    return lax.ppermute(value, axis, [(i, i ^ bit) for i in range(lax.axis_size(axis))])


slots = (0, 2, 1, 3)


def solution(mesh):
    nx, ny = mesh.shape["gx"], mesh.shape["gy"]
    square = nx == 4 and ny == 4

    def over_z(block):
        return block, flip(block, "gy", 2)

    def over_x(pair):
        block, far = pair
        mine = lax.axis_index("gx") // 2 == lax.axis_index("gy") // 2
        keep, give = jnp.where(mine, block, far), jnp.where(mine, far, block)
        return keep, flip(give, "gx", 2)

    def over_near_z(pair):
        keep = jnp.concatenate(pair)
        return keep, flip(keep, "gy", 1)

    def over_cores(pair):
        keep, near = pair
        mine = lax.axis_index("gx") % 2 == lax.axis_index("gy") % 2
        keep, give = jnp.where(mine, keep, near), jnp.where(mine, near, keep)
        return keep, flip(give, "gx", 1)

    def gather_plain(block):
        wide = lax.all_gather(block, "gy", axis=1, tiled=True)
        return lax.all_to_all(wide, "gx", split_axis=1, concat_axis=0, tiled=True)

    def sum_over_gx(partial, rows):
        if not square:
            return partial, lax.psum_scatter(partial, "gx", scatter_dimension=0, tiled=True)
        give = partial[2 * rows :]
        pair = partial[: 2 * rows] + flip(give.astype(jnp.bfloat16), "gx", 1).astype(jnp.float32)
        return pair, pair[:rows] + flip(pair[rows:].astype(jnp.bfloat16), "gx", 2).astype(jnp.float32)

    def local(layer_input, attn_context, ffn_hidden, norm_gain, w_query, w_keyval, w_out, w_down):
        rows, feat_width = layer_input.shape
        model_width = norm_gain.shape[0]

        input_float = layer_input.astype(jnp.float32)
        gain = lax.dynamic_slice_in_dim(norm_gain, lax.axis_index("gy") * feat_width, feat_width)
        own_sums = jnp.sum(input_float * input_float, axis=1)

        def normalise(row_sums):
            scale = lax.rsqrt(row_sums / model_width + norm_epsilon)
            return (input_float * scale[:, None] * gain).astype(jnp.bfloat16)

        if square:
            half = ffn_hidden.shape[1] // 2
            first, second = ffn_hidden[:, :half], ffn_hidden[:, half:]
            context, first = over_z(attn_context), over_z(first)
            sums = own_sums + flip(own_sums, "gy", 1)
            second = over_z(after(second, context[1]))
            sums = sums + flip(after(sums, context[1]), "gy", 2)
            context = over_x(context)
            normed = normalise(sums)
            ready_norm = normed
            normed = over_z(after(normed, second[1]))
            first = over_x(first)
            context = over_near_z(context)
            arrived = first[1]
            first = over_near_z(first)
            context = over_cores(context)
            block_part = dot(jnp.concatenate(after(context, arrived, ready_norm, second[1])), w_out)
            second = over_x(second)
            normed = over_x(after(normed, block_part))
            arrived = second[1]
            second = over_near_z(second)
            first = over_cores(after(first, arrived, block_part))
            block_part += dot(jnp.concatenate(first), w_down[:half])
            normed = over_near_z(after(normed, block_part))
            second = over_cores(after(second, block_part))
            block_part += dot(jnp.concatenate(second), w_down[half:])
            normed = jnp.concatenate(over_cores(after(normed, block_part)))
        else:
            normed = gather_plain(normalise(lax.psum(own_sums, "gy")))
            context, hidden = gather_plain(attn_context), gather_plain(ffn_hidden)
            block_part = dot(context, w_out) + dot(hidden, w_down)
        paired, block_sum = sum_over_gx(block_part, rows)
        normed = after(normed, paired)

        pieces = 2 if square else 1
        width = w_query.shape[1] // pieces
        heads = []
        for i in range(pieces):
            columns = dot(normed, w_query[:, i * width : (i + 1) * width])
            if i == 0:
                columns = jnp.concatenate([columns, dot(normed, w_keyval)], axis=1)
                normed = after(normed, columns, block_sum)
            heads.append(sum_over_gx(columns, rows)[1].astype(jnp.bfloat16))
        queries = jnp.concatenate([heads[0][:, :width], *heads[1:]], axis=1)
        return (queries, heads[0][:, width:], (input_float + block_sum).astype(jnp.bfloat16))

    return jax.shard_map(
        local,
        mesh=mesh,
        in_specs=(
            P(("groups", "gx"), "gy"),
            P(("groups", "gx"), "gy"),
            P(("groups", "gx"), "gy"),
            P(),
            P("gx", "gy"),
            P("gx", "gy"),
            P("gx", "gy"),
            P("gx", "gy"),
        ),
        out_specs=(P(("groups", "gx"), "gy"), P(("groups", "gx"), "gy"), P(("groups", "gx"), "gy")),
        check_vma=False,
    )
```

```python
import jax
import jax.numpy as jnp
from jax import lax
from jax.sharding import PartitionSpec as P

norm_epsilon = 1e-05


def after(value, *others):
    return lax.optimization_barrier((value, others))[0]


def dot(left, right):
    return jnp.dot(left, right, preferred_element_type=jnp.float32)


def flip(value, axis, bit):
    return lax.ppermute(value, axis, [(i, i ^ bit) for i in range(lax.axis_size(axis))])


slots = (0, 2, 1, 3)


def solution(mesh):
    nx, ny = mesh.shape["gx"], mesh.shape["gy"]
    square = nx == 4 and ny == 4

    def over_z(block):
        return block, flip(block, "gy", 2)

    def over_x(pair):
        block, far = pair
        mine = lax.axis_index("gx") // 2 == lax.axis_index("gy") // 2
        keep, give = jnp.where(mine, block, far), jnp.where(mine, far, block)
        return keep, flip(give, "gx", 2)

    def over_near_z(pair):
        keep = jnp.concatenate(pair)
        return keep, flip(keep, "gy", 1)

    def over_cores(pair):
        keep, near = pair
        mine = lax.axis_index("gx") % 2 == lax.axis_index("gy") % 2
        keep, give = jnp.where(mine, keep, near), jnp.where(mine, near, keep)
        return keep, flip(give, "gx", 1)

    def gather_plain(block):
        wide = lax.all_gather(block, "gy", axis=1, tiled=True)
        return lax.all_to_all(wide, "gx", split_axis=1, concat_axis=0, tiled=True)

    def sum_over_gx(partial, rows):
        if not square:
            return partial, lax.psum_scatter(partial, "gx", scatter_dimension=0, tiled=True)
        give = partial[2 * rows :]
        pair = partial[: 2 * rows] + flip(give.astype(jnp.bfloat16), "gx", 1).astype(jnp.float32)
        return pair, pair[:rows] + flip(pair[rows:].astype(jnp.bfloat16), "gx", 2).astype(jnp.float32)

    def local(layer_input, attn_context, ffn_hidden, norm_gain, w_query, w_keyval, w_out, w_down):
        rows, feat_width = layer_input.shape
        model_width = norm_gain.shape[0]

        input_float = layer_input.astype(jnp.float32)
        gain = lax.dynamic_slice_in_dim(norm_gain, lax.axis_index("gy") * feat_width, feat_width)
        own_sums = jnp.sum(input_float * input_float, axis=1)

        def normalise(row_sums):
            scale = lax.rsqrt(row_sums / model_width + norm_epsilon)
            return (input_float * scale[:, None] * gain).astype(jnp.bfloat16)

        if square:
            half = ffn_hidden.shape[1] // 2
            first, second = ffn_hidden[:, :half], ffn_hidden[:, half:]
            context, first = over_z(attn_context), over_z(first)
            sums = own_sums + flip(own_sums, "gy", 1)
            second = over_z(after(second, context[1]))
            sums = sums + flip(after(sums, context[1]), "gy", 2)
            context = over_x(context)
            normed = normalise(sums)
            ready_norm = normed
            normed = over_z(after(normed, second[1]))
            first = over_x(first)
            context = over_near_z(context)
            arrived = first[1]
            first = over_near_z(first)
            context = over_cores(context)
            block_part = dot(jnp.concatenate(after(context, arrived, ready_norm, second[1])), w_out)
            second = over_x(second)
            normed = over_x(after(normed, block_part))
            arrived = second[1]
            second = over_near_z(second)
            first = over_cores(after(first, arrived, block_part))
            block_part += dot(jnp.concatenate(after(first, arrived)), w_down[:half])
            normed = over_near_z(after(normed, block_part))
            second = over_cores(after(second, block_part))
            block_part += dot(jnp.concatenate(second), w_down[half:])
            normed = jnp.concatenate(over_cores(after(normed, block_part)))
        else:
            normed = gather_plain(normalise(lax.psum(own_sums, "gy")))
            context, hidden = gather_plain(attn_context), gather_plain(ffn_hidden)
            block_part = dot(context, w_out) + dot(hidden, w_down)
        paired, block_sum = sum_over_gx(block_part, rows)
        normed = after(normed, paired)

        pieces = 2 if square else 1
        width = w_query.shape[1] // pieces
        heads = []
        for i in range(pieces):
            columns = dot(normed, w_query[:, i * width : (i + 1) * width])
            if i == 0:
                columns = jnp.concatenate([columns, dot(normed, w_keyval)], axis=1)
                normed = after(normed, columns, block_sum)
            heads.append(sum_over_gx(columns, rows)[1])
        queries = jnp.concatenate([heads[0][:, :width], *heads[1:]], axis=1).astype(jnp.bfloat16)
        return (queries, heads[0][:, width:].astype(jnp.bfloat16), (input_float + block_sum).astype(jnp.bfloat16))

    return jax.shard_map(
        local,
        mesh=mesh,
        in_specs=(
            P(("groups", "gx"), "gy"),
            P(("groups", "gx"), "gy"),
            P(("groups", "gx"), "gy"),
            P(),
            P("gx", "gy"),
            P("gx", "gy"),
            P("gx", "gy"),
            P("gx", "gy"),
        ),
        out_specs=(P(("groups", "gx"), "gy"), P(("groups", "gx"), "gy"), P(("groups", "gx"), "gy")),
        check_vma=False,
    )
```
